512 devices in a mesh: dp: 32 (over z_lo, y), mp: 16 (over x, z_hi, core).
Axes of the slice: x: 4, y: 4, z: 16 (z_hi: 2, z_lo: 8; z = z_hi * 8 + z_lo), core: 2. Of those that a mesh axis runs over, the one named last changes fastest.
Arguments:
- cotangent: bfloat16 [16384, 6144], P('dp', 'mp'), may hold values from -24 to 24
- out_weight: bfloat16 [4096, 6144], P('mp'), may hold values from -0.09375 to 0.09375
- query_raw: bfloat16 [16384, 4096], P('dp', 'mp'), may hold values from -200 to 200
- key_raw: bfloat16 [16384, 4096], P('dp', 'mp'), may hold values from -200 to 200
- value: bfloat16 [16384, 4096], P('dp', 'mp'), may hold values from -6 to 6
- query_gain: float32 [32, 128], P('mp'), may hold values from 0.5 to 5
- key_gain: float32 [32, 128], P('mp'), may hold values from 0.5 to 5
Outputs:
- query_grad: bfloat16 [16384, 4096], P('dp', 'mp')
- key_grad: bfloat16 [16384, 4096], P('dp', 'mp')
- value_gradient: bfloat16 [16384, 4096], P('dp', 'mp')
- out_weight_grad: bfloat16 [4096, 6144], P(('mp', 'dp'))
- query_gain_grad: float32 [32, 128], P('mp')
- key_gain_grad: float32 [32, 128], P('mp')
The draws below stay inside these ranges and needn't reach their ends.
All inputs are finite; a program needn't handle non-finite values.
Results may differ from the reference program's by a relative error of at most 0.03.
The reference program's roundings to bfloat16 on the way count: a program that leaves them out, or rounds other values in their place, can miss the bound.
Values may be sent and summed in bfloat16 or wider, within the bound.
A program may use at most 64 MiB of HBM per device.

```python
import math
import jax
import jax.numpy as jnp
from jax import lax

D = 6144
HEADS = 32
HEAD_DIM = 128
PATCHES = 256
TOK_DEV = 512
TOKENS = 16384
N_DP = 32


def raw_pair(key, copy_rows):
    columns_total = HEADS * HEAD_DIM
    array_shape = (TOKENS, columns_total)
    subkeys = jax.random.split(key, 7)

    def sample_base(seed_key):
        gauss = jnp.clip(jax.random.normal(seed_key, array_shape, jnp.float32), -4.0, 4.0)
        return gauss
    rows_query = jnp.exp(jax.random.uniform(subkeys[2], (TOKENS, 1), jnp.float32, 0.0, math.log(10.0)))
    cols_query = jnp.exp(jax.random.uniform(subkeys[3], (1, columns_total), jnp.float32, 0.0, math.log(4.0)))
    rows_key = jnp.exp(jax.random.uniform(subkeys[4], (TOKENS, 1), jnp.float32, 0.0, math.log(10.0)))
    cols_key = jnp.exp(jax.random.uniform(subkeys[5], (1, columns_total), jnp.float32, 0.0, math.log(4.0)))
    query_drawn = sample_base(subkeys[0]) * rows_query * cols_query
    keys_drawn = sample_base(subkeys[1]) * rows_key * cols_key
    jitter = jnp.clip(jax.random.normal(subkeys[6], array_shape, jnp.float32), -4.0, 4.0) * 0.08 * rows_query * cols_query
    position = jnp.arange(TOKENS) % PATCHES
    spacing = max(PATCHES // 4, 4)
    copy_one = (position % spacing == 1)[:, None] & (copy_rows > 0.5)
    copy_two = (position % spacing == 2)[:, None] & (copy_rows > 0.5)
    keys_drawn = jnp.where(copy_one, jnp.roll(query_drawn, 1, axis=0), keys_drawn)
    keys_drawn = jnp.where(copy_two, jnp.roll(query_drawn + jitter, 2, axis=0), keys_drawn)
    return (query_drawn, keys_drawn)


def draw_query_raw(key, part):
    drawn = raw_pair(key, 0.0)
    return drawn[0].astype(jnp.bfloat16)


def draw_key_raw(key, part):
    drawn = raw_pair(key, 0.0)
    return drawn[1].astype(jnp.bfloat16)


def draw_query_gain(key, part):
    key = jax.random.fold_in(key, 11)
    return jnp.exp(jax.random.uniform(key, (HEADS, HEAD_DIM), jnp.float32, math.log(0.5), math.log(2.0)))


def draw_key_gain(key, part):
    key = jax.random.fold_in(key, 23)
    return jnp.exp(jax.random.uniform(key, (HEADS, HEAD_DIM), jnp.float32, math.log(0.5), math.log(2.0)))


def steps_of(own_key, dims, cuts, low, top_value):
    def one(dim, blocks):
        draws = jax.random.uniform(jax.random.fold_in(jax.random.fold_in(own_key, 6), dim), (blocks,), jnp.float32, low / len(cuts), top_value / len(cuts))
        return jnp.repeat(jnp.exp(draws), dims[dim] // blocks).reshape((-1,) + (1,) * (len(dims) - dim - 1))

    level = one(*cuts[0])
    for cut in cuts[1:]:
        level = level * one(*cut)
    return level


def centred(rng, shape, deviation, bound, shards=(), held_as=jnp.bfloat16):
    factor_of = steps_of(rng, shape, shards, -0.22, 0.18) if shards else 1.0
    result = jax.random.normal(rng, shape, jnp.float32) * deviation * factor_of
    return jnp.minimum(jnp.maximum(result, -bound), bound).astype(held_as)


def setup_inputs(seed: int = 0) -> dict:
    seeds = jax.random.split(jax.random.key(seed), 8)
    cotangent = centred(seeds[0], (TOKENS, D), 4.0, 24.0, ((0, 32), (1, 16)))
    out_weight = centred(seeds[1], (HEADS * HEAD_DIM, D), (HEADS * HEAD_DIM) ** -0.5, 0.09375, ((0, 16),))
    query_raw = draw_query_raw(jax.random.fold_in(seeds[7], 71), 0)
    key_raw = draw_key_raw(jax.random.fold_in(seeds[7], 71), 0)
    value = centred(seeds[4], (TOKENS, HEADS * HEAD_DIM), 1.0, 6.0, ((0, 32), (1, 16)))
    query_gain = draw_query_gain(jax.random.fold_in(seeds[7], 71), 0)
    key_gain = draw_key_gain(jax.random.fold_in(seeds[7], 71), 0)
    return dict(cotangent=cotangent, out_weight=out_weight, query_raw=query_raw, key_raw=key_raw, value=value, query_gain=query_gain, key_gain=key_gain)


EPSILON = 1e-06

def normalize(raw_values):
    floats = raw_values.astype(jnp.float32)
    center = floats - lax.optimization_barrier(jnp.mean(floats, axis=-1, keepdims=True))
    inverse = lax.rsqrt(lax.optimization_barrier(jnp.mean(center * center, axis=-1, keepdims=True)) + EPSILON)
    return (center * inverse, inverse)

def norm_backward(upstream, normed, inverse, gain_row):
    scaled = upstream * gain_row
    centered = scaled - lax.optimization_barrier(jnp.mean(scaled, axis=-1, keepdims=True))
    return inverse * (centered - normed * lax.optimization_barrier(jnp.mean(scaled * normed, axis=-1, keepdims=True)))

def head_backward(inputs):
    query_head, key_head, value_head, grad_head, query_scale, key_scale = inputs
    images = TOKENS // PATCHES
    head_shape = (images, PATCHES, HEAD_DIM)
    score_factor = HEAD_DIM ** (-0.5)
    query_norm, query_inverse = normalize(query_head.reshape(head_shape))
    key_norm, key_inverse = normalize(key_head.reshape(head_shape))
    query_applied = (query_norm * query_scale).astype(jnp.bfloat16)
    key_applied = (key_norm * key_scale).astype(jnp.bfloat16)
    attention_scores = jnp.einsum('spr,sfr->spf', query_applied.astype(jnp.float32), key_applied.astype(jnp.float32)) * score_factor
    probs = jax.nn.softmax(attention_scores, axis=-1)
    probability_reduced = probs.astype(jnp.bfloat16).astype(jnp.float32)
    value_three_axes = value_head.reshape(head_shape).astype(jnp.float32)
    gradient_three_axes = grad_head.reshape(head_shape).astype(jnp.float32)
    attended_values = jnp.einsum('tzp,tpe->tze', probability_reduced, value_three_axes).astype(jnp.bfloat16)
    value_gradient = jnp.einsum('rlz,rle->rze', probability_reduced, gradient_three_axes).astype(jnp.bfloat16)
    probability_gradient = jnp.einsum('spr,sfr->spf', gradient_three_axes, value_three_axes)
    row_dot = lax.optimization_barrier(jnp.sum(probs * probability_gradient, axis=-1, keepdims=True))
    score_gradient = (probs * (probability_gradient - row_dot) * score_factor).astype(jnp.bfloat16).astype(jnp.float32)
    query_applied_gradient = jnp.einsum('tzp,tpe->tze', score_gradient, key_applied.astype(jnp.float32))
    key_applied_gradient = jnp.einsum('rlz,rle->rze', score_gradient, query_applied.astype(jnp.float32))
    query_gain_grad = lax.optimization_barrier(jnp.sum(lax.optimization_barrier(jnp.sum((query_applied_gradient * query_norm).reshape(N_DP, -1, HEAD_DIM), axis=1)) / N_DP, axis=0))
    key_gain_grad = lax.optimization_barrier(jnp.sum(lax.optimization_barrier(jnp.sum((key_applied_gradient * key_norm).reshape(N_DP, -1, HEAD_DIM), axis=1)) / N_DP, axis=0))
    query_grad = norm_backward(query_applied_gradient, query_norm, query_inverse, query_scale).astype(jnp.bfloat16)
    key_grad = norm_backward(key_applied_gradient, key_norm, key_inverse, key_scale).astype(jnp.bfloat16)
    return (attended_values.reshape(TOKENS, HEAD_DIM), query_grad.reshape(TOKENS, HEAD_DIM), key_grad.reshape(TOKENS, HEAD_DIM), value_gradient.reshape(TOKENS, HEAD_DIM), query_gain_grad, key_gain_grad)

def split_heads(matrix):
    return matrix.reshape(TOKENS, HEADS, HEAD_DIM).transpose(1, 0, 2)

def join_heads(matrix):
    return matrix.transpose(1, 0, 2).reshape(TOKENS, HEADS * HEAD_DIM)

def add_group(running_sum, group_pair):
    attended_group, cotangent_group = group_pair
    partial_value = lax.dot_general(attended_group, cotangent_group, (((0,), (0,)), ((), ())), preferred_element_type=jnp.float32) / N_DP
    rounded = lax.optimization_barrier(partial_value.astype(jnp.bfloat16))
    return (running_sum + rounded.astype(jnp.float32), None)

def reference(cotangent, out_weight, query_raw, key_raw, value, query_gain, key_gain):
    attn_grad = jnp.dot(cotangent, out_weight.T, preferred_element_type=jnp.float32).astype(jnp.bfloat16)
    results = lax.map(head_backward, (split_heads(query_raw), split_heads(key_raw), split_heads(value), split_heads(attn_grad), query_gain, key_gain))
    attended_values = join_heads(results[0])
    start_sum = jnp.zeros((HEADS * HEAD_DIM, D), jnp.float32)
    weight_sum, unused = lax.scan(add_group, start_sum, (attended_values.reshape(N_DP, TOK_DEV, HEADS * HEAD_DIM), cotangent.reshape(N_DP, TOK_DEV, D)))
    return (join_heads(results[1]), join_heads(results[2]), join_heads(results[3]), weight_sum.astype(jnp.bfloat16), results[4], results[5])
```

```python
import jax
import jax.numpy as jnp
from jax import lax
from jax.experimental import pallas as pl
from jax.experimental.pallas import tpu as pltpu
from jax.sharding import PartitionSpec as P

MESH = pl.DeviceIdType.MESH
F32 = jnp.float32
BF16 = jnp.bfloat16

PATCHES = 256
HEAD = 128
EPSILON = 1e-06
TOK = 512
LANES = 128
CHIPS = 8
BLOCKS = 3
UNITS = CHIPS * BLOCKS
HALF = UNITS // 2
GROUP = 6
AHEAD = 2
BEHIND = 3
NY = 4
NZ = 8
ROWS = 16

NT = (((1,), (1,)), ((), ()))
TN = (((0,), (0,)), ((), ()))


def dot(a, b, dims=(((1,), (0,)), ((), ()))):
    return lax.dot_general(a, b, dims, preferred_element_type=F32)


def normalize(raw):
    floats = raw.astype(F32)
    center = floats - jnp.mean(floats, axis=-1, keepdims=True)
    inverse = lax.rsqrt(jnp.mean(center * center, axis=-1, keepdims=True) + EPSILON)
    return center * inverse, inverse


def norm_backward(upstream, normed, inverse, gain):
    scaled = upstream * gain
    centered = scaled - jnp.mean(scaled, axis=-1, keepdims=True)
    return inverse * (centered - normed * jnp.mean(scaled * normed, axis=-1, keepdims=True))


def kernel(
    cot_hbm, w_hbm, q_hbm, k_hbm, v_hbm, qg_ref, kg_ref,
    qgrad_ref, kgrad_ref, vgrad_ref, wgrad_ref, qgg_ref, kgg_ref,
    ag, w, qraw, kraw, v, qn, kn, qinv, kinv, qu, ku, probs, att, acc,
    ysend, yrecv, zsend, zrecv, gown, gy, gsum, gz,
    local_sem, send_sem, x_sem, core_sem, y_sem, z_sem, g_sem,
):
    d = lax.axis_index("dp")
    m = lax.axis_index("mp")
    y = lax.rem(d, NY)
    zl = d // NY
    x = m // 4
    zh = lax.rem(m // 2, 2)
    c = lax.rem(m, 2)

    def x_peer(k):
        return (d, lax.rem(x + k, 4) * 4 + zh * 2 + c)

    def y_peer(k):
        return (zl * NY + lax.rem(y + k, NY), m)

    def z_peer(k):
        return (lax.rem(zl + k, NZ) * NY + y, m)

    core_peer = (d, m + 1 - 2 * c)
    far_peer = (d, x * 4 + (1 - zh) * 2 + c)

    barrier = pltpu.get_barrier_semaphore()
    peers = [far_peer, core_peer]
    peers += [x_peer(k) for k in (1, 2, 3)]
    peers += [y_peer(k) for k in (1, 2, 3)]
    peers += [z_peer(k) for k in range(1, NZ)]
    for peer in peers:
        pl.semaphore_signal(barrier, inc=1, device_id=peer, device_id_type=MESH)

    loads = [
        pltpu.make_async_copy(q_hbm, qraw, local_sem.at[0]),
        pltpu.make_async_copy(k_hbm, kraw, local_sem.at[1]),
        pltpu.make_async_copy(v_hbm, v, local_sem.at[2]),
    ]
    for j in range(BLOCKS):
        loads.append(
            pltpu.make_async_copy(
                cot_hbm.at[:, pl.ds(j * LANES, LANES)], ag.at[0, j, c], local_sem.at[3 + j]
            )
        )
    loads.append(pltpu.make_async_copy(w_hbm, w, local_sem.at[3 + BLOCKS]))
    for load in loads:
        load.start()
    for load in loads[:3]:
        load.wait()

    factor = HEAD ** (-0.5)
    acc[...] = jnp.zeros_like(acc)

    for image in range(2):
        for head in range(2):
            pair = image * 2 + head
            rows = pl.ds(image * PATCHES, PATCHES)
            cols = pl.ds(head * HEAD, HEAD)
            normed, inverse = normalize(qraw[rows, cols])
            qn[pair] = normed
            qinv[pair] = inverse
            query = (normed * qg_ref[pl.ds(head, 1), :]).astype(BF16)
            qu[pair] = query
            normed, inverse = normalize(kraw[rows, cols])
            kn[pair] = normed
            kinv[pair] = inverse
            keys = (normed * kg_ref[pl.ds(head, 1), :]).astype(BF16)
            ku[pair] = keys
            scores = dot(keys, query, NT) * factor
            weights = jnp.exp(scores - jnp.max(scores, axis=0, keepdims=True))
            weights = weights / jnp.sum(weights, axis=0, keepdims=True)
            probs[pair] = weights
            attended = dot(v[rows, cols], weights.astype(BF16), TN)
            att[cols, rows] = attended.astype(BF16)

    for load in loads[3:]:
        load.wait()
    pl.semaphore_wait(barrier, len(peers))

    def remote(src, dst, sent, landed, peer):
        return pltpu.make_async_remote_copy(
            src_ref=src, dst_ref=dst, send_sem=sent, recv_sem=landed,
            device_id=peer, device_id_type=MESH,
        )

    def send_x(slot, j):
        for k in (1, 3, 2):
            remote(
                ag.at[slot, j, c], ag.at[slot + 4 - k, j, c],
                send_sem.at[1], x_sem.at[slot + 4 - k, j], x_peer(k),
            ).start()

    def send_core(slot, j):
        remote(
            ag.at[slot, j, c], ag.at[slot, j, c],
            send_sem.at[2], core_sem.at[slot, j], core_peer,
        ).start()

    for j in range(BLOCKS):
        remote(ag.at[0, j, c], ag.at[4, j, c], send_sem.at[0], x_sem.at[4, j], far_peer).start()
        send_core(0, j)
        send_x(0, j)

    def place(unit):
        half = unit // HALF
        rest = lax.rem(unit, HALF)
        return half, rest // 4, half * 4 + lax.rem(rest, 4)

    def await_block(slot, j, sem):
        pltpu.make_async_copy(ag.at[slot, j, 0], ag.at[slot, j, 0], sem).wait()

    def forward(unit):
        half, j, slot = place(unit)

        @pl.when(slot != 0)
        def _():
            await_block(slot, j, x_sem.at[slot, j])

            @pl.when(slot == 4)
            def _():
                send_x(4, j)

            send_core(slot, j)

    def column(unit):
        half, j, slot = place(unit)
        owner = lax.rem(x + lax.rem(slot, 4), 4) * 2 + lax.rem(zh + half, 2)
        return pl.multiple_of(owner * 768 + j * LANES, LANES)

    def project(unit):
        half, j, slot = place(unit)
        await_block(slot, j, core_sem.at[slot, j])
        start = column(unit)
        weight = jnp.concatenate(
            [w[:, pl.ds(start, LANES)], w[:, pl.ds(start + 384, LANES)]], axis=1
        )
        for part in range(2):
            rows = pl.ds(part * 256, 256)
            block = jnp.concatenate([ag[slot, j, 0, rows, :], ag[slot, j, 1, rows, :]], axis=1)
            acc[rows, :] += dot(block, weight, NT)
        block = jnp.concatenate([ag[slot, j, 0], ag[slot, j, 1]], axis=1)
        terms = dot(att[...], block) * (1.0 / 32.0)
        first = terms[:, :LANES].reshape(NZ, NY, 8, LANES)
        second = terms[:, LANES:].reshape(NZ, NY, 8, LANES)
        both = jnp.concatenate([first, second], axis=2).astype(BF16)
        for part in range(NY):
            ysend[unit, part] = both[:, part]
        for k in (1, 3, 2):
            remote(
                ysend.at[unit, lax.rem(y + k, NY)], yrecv.at[unit, k - 1],
                send_sem.at[3], y_sem.at[unit], y_peer(k),
            ).start()

    def sum_y(unit):
        pltpu.make_async_copy(yrecv.at[unit], yrecv.at[unit], y_sem.at[unit]).wait()
        total = ysend[unit, y].astype(F32)
        for k in range(3):
            total += yrecv[unit, k].astype(F32)
        zsend[:, unit] = total.astype(BF16)

    def send_z(group):
        span = pl.ds(group * GROUP, GROUP)
        for k in range(1, NZ):
            remote(
                zsend.at[lax.rem(zl + k, NZ), span], zrecv.at[zl, span],
                send_sem.at[4], z_sem.at[group], z_peer(k),
            ).start()

    for unit in range(AHEAD):
        forward(jnp.int32(unit))

    @pl.loop(0, UNITS)
    def _(unit):
        @pl.when(unit + AHEAD < UNITS)
        def _():
            forward(unit + AHEAD)

        project(unit)

        @pl.when(unit >= BEHIND)
        def _():
            sum_y(unit - BEHIND)

            @pl.when(lax.rem(unit - BEHIND, GROUP) == GROUP - 1)
            def _():
                send_z((unit - BEHIND) // GROUP)

    gains = [[None, None], [None, None]]

    def backward(image, head):
        pair = image * 2 + head
        rows = pl.ds(image * PATCHES, PATCHES)
        cols = pl.ds(head * HEAD, HEAD)
        grad = acc[rows, cols].astype(BF16)
        weights = probs[pair]
        vgrad_ref[rows, cols] = dot(weights.astype(BF16), grad).astype(BF16)
        upstream = dot(v[rows, cols], grad, NT)
        row_dot = jnp.sum(weights * upstream, axis=0, keepdims=True)
        score = (weights * (upstream - row_dot) * factor).astype(BF16)
        kup = dot(score, qu[pair])
        qup = dot(score, ku[pair], TN)
        for which, (up, normed, inverse, gain, out) in enumerate((
            (qup, qn[pair], qinv[pair], qg_ref[pl.ds(head, 1), :], qgrad_ref),
            (kup, kn[pair], kinv[pair], kg_ref[pl.ds(head, 1), :], kgrad_ref),
        )):
            part = jnp.sum(up * normed, axis=0, keepdims=True)
            old = gains[which][head]
            gains[which][head] = part if old is None else old + part
            out[rows, cols] = norm_backward(up, normed, inverse, gain).astype(BF16)

    backward(0, 0)
    backward(0, 1)
    for unit in range(UNITS - BEHIND, UNITS):
        sum_y(unit)
    send_z(UNITS // GROUP - 1)
    backward(1, 0)
    backward(1, 1)

    gown[...] = jnp.zeros_like(gown)
    for which in range(2):
        for head in range(2):
            gown[pl.ds(which * 2 + head, 1), :] = gains[which][head] * (1.0 / 32.0)
    for k in (1, 2, 3):
        remote(gown, gy.at[k - 1], send_sem.at[5], g_sem.at[0], y_peer(k)).start()
    pltpu.make_async_copy(gy, gy, g_sem.at[0]).wait()
    gsum[...] = gown[...] + gy[0] + gy[1] + gy[2]
    for k in range(1, NZ):
        remote(gsum, gz.at[k - 1], send_sem.at[6], g_sem.at[1], z_peer(k)).start()

    zrecv[zl] = zsend[zl]
    for group in range(UNITS // GROUP):
        span = pl.ds(group * GROUP, GROUP)
        landed = zrecv.at[pl.ds(0, NZ - 1), span]
        pltpu.make_async_copy(landed, landed, z_sem.at[group]).wait()

    @pl.loop(0, UNITS)
    def _(unit):
        total = zrecv[0, unit].astype(F32)
        for k in range(1, NZ):
            total += zrecv[k, unit].astype(F32)
        total = total.astype(BF16)
        start = column(unit)
        wgrad_ref[:, pl.ds(start, LANES)] = total[:8]
        wgrad_ref[:, pl.ds(start + 384, LANES)] = total[8:]

    pltpu.make_async_copy(gz, gz, g_sem.at[1]).wait()
    total = gsum[...]
    for k in range(NZ - 1):
        total += gz[k]
    qgg_ref[...] = total[0:2]
    kgg_ref[...] = total[2:4]

    pltpu.make_async_copy(ag.at[0, :, 0], ag.at[0, :, 0], send_sem.at[0]).wait()
    pltpu.make_async_copy(ag.at[pl.ds(0, 3)], ag.at[pl.ds(0, 3)], send_sem.at[1]).wait()
    pltpu.make_async_copy(ag.at[pl.ds(0, 4)], ag.at[pl.ds(0, 4)], send_sem.at[2]).wait()
    pltpu.make_async_copy(yrecv, yrecv, send_sem.at[3]).wait()
    sent = zrecv.at[pl.ds(0, NZ - 1)]
    pltpu.make_async_copy(sent, sent, send_sem.at[4]).wait()
    pltpu.make_async_copy(gy, gy, send_sem.at[5]).wait()
    pltpu.make_async_copy(gz, gz, send_sem.at[6]).wait()


def local(cotangent, out_weight, query_raw, key_raw, value, query_gain, key_gain):
    anywhere = pl.BlockSpec(memory_space=pl.ANY)
    vmem = pl.BlockSpec(memory_space=pltpu.VMEM)
    pair = (4, PATCHES, HEAD)
    outs = pl.pallas_call(
        kernel,
        out_shape=(
            jax.ShapeDtypeStruct((TOK, 256), BF16),
            jax.ShapeDtypeStruct((TOK, 256), BF16),
            jax.ShapeDtypeStruct((TOK, 256), BF16),
            jax.ShapeDtypeStruct((8, 6144), BF16),
            jax.ShapeDtypeStruct((2, HEAD), F32),
            jax.ShapeDtypeStruct((2, HEAD), F32),
        ),
        in_specs=[anywhere] * 5 + [vmem] * 2,
        out_specs=[vmem] * 6,
        scratch_shapes=[
            pltpu.VMEM((CHIPS, BLOCKS, 2, TOK, LANES), BF16),
            pltpu.VMEM((256, 6144), BF16),
            pltpu.VMEM((TOK, 256), BF16),
            pltpu.VMEM((TOK, 256), BF16),
            pltpu.VMEM((TOK, 256), BF16),
            pltpu.VMEM(pair, F32),
            pltpu.VMEM(pair, F32),
            pltpu.VMEM((4, PATCHES, 1), F32),
            pltpu.VMEM((4, PATCHES, 1), F32),
            pltpu.VMEM(pair, BF16),
            pltpu.VMEM(pair, BF16),
            pltpu.VMEM((4, PATCHES, PATCHES), F32),
            pltpu.VMEM((256, TOK), BF16),
            pltpu.VMEM((TOK, 256), F32),
            pltpu.VMEM((UNITS, NY, NZ, ROWS, LANES), BF16),
            pltpu.VMEM((UNITS, NY - 1, NZ, ROWS, LANES), BF16),
            pltpu.VMEM((NZ, UNITS, ROWS, LANES), BF16),
            pltpu.VMEM((NZ, UNITS, ROWS, LANES), BF16),
            pltpu.VMEM((8, LANES), F32),
            pltpu.VMEM((NY - 1, 8, LANES), F32),
            pltpu.VMEM((8, LANES), F32),
            pltpu.VMEM((NZ - 1, 8, LANES), F32),
            pltpu.SemaphoreType.DMA((4 + BLOCKS,)),
            pltpu.SemaphoreType.DMA((7,)),
            pltpu.SemaphoreType.DMA((CHIPS, BLOCKS)),
            pltpu.SemaphoreType.DMA((CHIPS, BLOCKS)),
            pltpu.SemaphoreType.DMA((UNITS,)),
            pltpu.SemaphoreType.DMA((UNITS // GROUP,)),
            pltpu.SemaphoreType.DMA((2,)),
        ],
        compiler_params=pltpu.CompilerParams(
            collective_id=0, has_side_effects=True, vmem_limit_bytes=48 << 20
        ),
        cost_estimate=pl.CostEstimate(
            flops=4 * 10**9, bytes_accessed=6 * 10**6, transcendentals=4 * 65536
        ),
        name="attention_backward",
    )(cotangent, out_weight, query_raw, key_raw, value, query_gain, key_gain)
    return tuple(outs)


def solution(mesh):
    return jax.shard_map(
        local,
        mesh=mesh,
        in_specs=(
            P("dp", "mp"),
            P("mp", None),
            P("dp", "mp"),
            P("dp", "mp"),
            P("dp", "mp"),
            P("mp", None),
            P("mp", None),
        ),
        out_specs=(
            P("dp", "mp"),
            P("dp", "mp"),
            P("dp", "mp"),
            P(("mp", "dp"), None),
            P("mp", None),
            P("mp", None),
        ),
        check_vma=False,
    )
```

```python
import jax
import jax.numpy as jnp
from jax import lax
from jax.experimental import pallas as pl
from jax.experimental.pallas import tpu as pltpu
from jax.sharding import PartitionSpec as P

MESH = pl.DeviceIdType.MESH
F32 = jnp.float32
BF16 = jnp.bfloat16

PATCHES = 256
HEAD = 128
EPSILON = 1e-06
TOK = 512
LANES = 128
CHIPS = 8
BLOCKS = 3
UNITS = CHIPS * BLOCKS // 2
GROUP = 2
GROUPS = UNITS // GROUP
NY = 4
NZ = 8
ROWS = 16
REVERSED = (0, 4, 2, 6, 1, 5, 3, 7)

NT = (((1,), (1,)), ((), ()))
TN = (((0,), (0,)), ((), ()))


def dot(a, b, dims=(((1,), (0,)), ((), ()))):
    return lax.dot_general(a, b, dims, preferred_element_type=F32)


def normalize(raw):
    floats = raw.astype(F32)
    center = floats - jnp.mean(floats, axis=-1, keepdims=True)
    inverse = lax.rsqrt(jnp.mean(center * center, axis=-1, keepdims=True) + EPSILON)
    return center * inverse, inverse


def norm_backward(upstream, normed, inverse, gain):
    scaled = upstream * gain
    centered = scaled - jnp.mean(scaled, axis=-1, keepdims=True)
    return inverse * (centered - normed * jnp.mean(scaled * normed, axis=-1, keepdims=True))


def kernel(
    cot_hbm, w_hbm, q_hbm, k_hbm, v_hbm, qg_ref, kg_ref,
    qgrad_ref, kgrad_ref, vgrad_ref, wgrad_ref, qgg_ref, kgg_ref,
    ag, transit, w2, qraw, kraw, v, qn, kn, qinv, kinv, qu, ku, probs, att, acc, accr,
    ysend, yrecv, z0, r0, z1, r1, z2, r2, wsend, wrecv, gown, gy, gsum, gz,
    local_sem, send_sem, leg_sem, far_sem, x_sem, core_sem, acc_sem, out_sem, y1_sem, y_sem, z_sem, gy_sem, gz_sem,
):
    d = lax.axis_index("dp")
    m = lax.axis_index("mp")
    y = lax.rem(d, NY)
    zl = d // NY
    x = m // 4
    zh = lax.rem(m // 2, 2)
    c = lax.rem(m, 2)
    z = zh * NZ + zl
    bits = [lax.rem(zl // step, 2) for step in (1, 2, 4)]

    def x_peer(k):
        return (d, lax.rem(x + k, 4) * 4 + zh * 2 + c)

    def y_peer(k):
        return (zl * NY + lax.rem(y + k, NY), m)

    def z_peer(k):
        other = lax.rem(z + k, 2 * NZ)
        return (lax.rem(other, NZ) * NY + y, x * 4 + (other // NZ) * 2 + c)

    def half_peer(stage):
        step = 1 << stage
        return ((zl + step - 2 * step * bits[stage]) * NY + y, m)

    core_peer = (d, m + 1 - 2 * c)

    barrier = pltpu.get_barrier_semaphore()
    peers = [z_peer(4), z_peer(12), core_peer, half_peer(0), half_peer(1)]
    peers += [x_peer(k) for k in (1, 3)]
    peers += [y_peer(k) for k in (1, 2, 3)]
    for peer in peers:
        pl.semaphore_signal(barrier, inc=1, device_id=peer, device_id_type=MESH)

    loads = [
        pltpu.make_async_copy(q_hbm, qraw, local_sem.at[0]),
        pltpu.make_async_copy(k_hbm, kraw, local_sem.at[1]),
        pltpu.make_async_copy(v_hbm, v, local_sem.at[2]),
    ]
    for j in range(BLOCKS):
        loads.append(
            pltpu.make_async_copy(
                cot_hbm.at[:, pl.ds(j * LANES, LANES)], ag.at[0, j], local_sem.at[3 + j]
            )
        )
    for chip in range(CHIPS):
        start = pl.multiple_of(chip * 768 + c * 384, LANES)
        loads.append(
            pltpu.make_async_copy(
                w_hbm.at[:, pl.ds(start, 384)], w2.at[c, chip], local_sem.at[3 + BLOCKS]
            )
        )
    for load in loads:
        load.start()

    def remote(src, dst, sent, landed, peer):
        return pltpu.make_async_remote_copy(
            src_ref=src, dst_ref=dst, send_sem=sent, recv_sem=landed,
            device_id=peer, device_id_type=MESH,
        )

    def landed(ref, sem):
        pltpu.make_async_copy(ref, ref, sem).wait()

    def send_x(slot, j):
        for k in (1, 3):
            remote(
                ag.at[slot, j], ag.at[slot + 4 - k, j],
                send_sem.at[1], x_sem.at[slot + 4 - k, j], x_peer(k),
            ).start()

    def part(p):
        return pl.ds(p * 256, 256)

    factor = HEAD ** (-0.5)

    def forward(image, head):
        pair = image * 2 + head
        rows = pl.ds(image * PATCHES, PATCHES)
        cols = pl.ds(head * HEAD, HEAD)
        normed, inverse = normalize(qraw[rows, cols])
        qn[pair] = normed
        qinv[pair] = inverse
        query = (normed * qg_ref[pl.ds(head, 1), :]).astype(BF16)
        qu[pair] = query
        normed, inverse = normalize(kraw[rows, cols])
        kn[pair] = normed
        kinv[pair] = inverse
        keys = (normed * kg_ref[pl.ds(head, 1), :]).astype(BF16)
        ku[pair] = keys
        scores = dot(keys, query, NT) * factor
        weights = jnp.exp(scores - jnp.max(scores, axis=0, keepdims=True))
        weights = weights / jnp.sum(weights, axis=0, keepdims=True)
        probs[pair] = weights
        attended = dot(v[rows, cols], weights.astype(BF16), TN)
        att[c, cols, rows] = attended.astype(BF16)

    for load in loads[:3]:
        load.wait()
    forward(0, 0)
    forward(0, 1)
    for load in loads[3:3 + BLOCKS]:
        load.wait()
    pl.semaphore_wait(barrier, len(peers))
    def send_leg(j):
        for p in range(2):
            remote(
                ag.at[0, j, part(p)], transit.at[j, p],
                send_sem.at[0], leg_sem.at[j, p], z_peer(4 + 8 * p),
            ).start()

    send_leg(0)
    send_leg(1)
    for j in range(BLOCKS):
        send_x(0, j)
    for chip in range(CHIPS):
        start = pl.multiple_of(chip * 768 + (1 - c) * 384, LANES)
        remote(
            w_hbm.at[:, pl.ds(start, 384)], w2.at[c, chip],
            send_sem.at[2], core_sem.at[0], core_peer,
        ).start()
    forward(1, 0)
    forward(1, 1)
    remote(att.at[c], att.at[c], send_sem.at[11], core_sem.at[1], core_peer).start()
    acc[...] = jnp.zeros_like(acc)
    landed(w2.at[c], local_sem.at[3 + BLOCKS])

    def arrive_weights():
        landed(w2.at[1 - c], core_sem.at[0])
        landed(att.at[1 - c], core_sem.at[1])

    def pass_on(j):
        for p in range(2):
            landed(transit.at[j, p], leg_sem.at[j, p])
            remote(
                transit.at[j, p], ag.at[4, j, part(p)],
                send_sem.at[0], far_sem.at[j, p], z_peer(4 + 8 * p),
            ).start()
        if j == 0:
            send_leg(2)

    def arrive_far(j):
        for p in range(2):
            landed(ag.at[4, j, part(p)], far_sem.at[j, p])
        send_x(4, j)

    def arrive_near(group):
        half, j = divmod(group, BLOCKS)
        for k, p in ((1, 1), (3, 0)):
            slot = half * 4 + k
            landed(ag.at[slot, j], x_sem.at[slot, j])
            remote(
                ag.at[slot, j, part(p)], ag.at[half * 4 + 2, j, part(p)],
                send_sem.at[1], x_sem.at[half * 4 + 2, j], x_peer(4 - k),
            ).start()

    def arrive_opposite(group):
        slot = (group // BLOCKS) * 4 + 2
        j = lax.rem(group, BLOCKS)
        landed(ag.at[slot, j], x_sem.at[slot, j])

    def place(unit):
        group = unit // GROUP
        half = group // BLOCKS
        near = 1 - lax.rem(unit, GROUP)
        owners = [
            lax.rem(x + near + k, 4) * 2 + lax.rem(zh + half, 2) for k in (0, 2)
        ]
        return half * 4 + near, owners, lax.rem(group, BLOCKS)

    def column(owner, core, j):
        return pl.multiple_of(owner * 768 + core * 384 + j * LANES, LANES)

    up, across, down = [lax.rem(y + k, NY) for k in (1, 2, 3)]

    def quads(p):
        return pl.ds(p * 4, 4)

    def send_y(unit, to, p, slot, sem, k):
        remote(
            ysend.at[unit, to, quads(p)], yrecv.at[unit, slot, quads(p)],
            send_sem.at[3], sem.at[unit], y_peer(k),
        ).start()

    def project(unit):
        slot, owners, j = place(unit)
        cols = pl.ds(pl.multiple_of(j * LANES, LANES), LANES)
        block = jnp.concatenate([ag[slot, j], ag[slot + 2, j]], axis=1)
        terms = [
            (dot(att[core], block) * (1.0 / 32.0)).reshape(NZ, NY, 8, 2 * LANES)
            for core in range(2)
        ]
        both = jnp.concatenate(terms, axis=2).astype(BF16)
        for to in range(NZ):
            for p in range(NY):
                for k in range(2):
                    ysend[unit, p, REVERSED[to], k] = both[to, p, :, k * LANES:(k + 1) * LANES]
        send_y(unit, across, 0, 0, y1_sem, 1)
        send_y(unit, across, 1, 0, y1_sem, 3)
        send_y(unit, up, 1, 1, y_sem, 1)
        send_y(unit, down, 0, 2, y_sem, 3)
        for core in range(2):
            weight = jnp.concatenate([w2[core, owner, :, cols] for owner in owners], axis=1)
            for p in range(2):
                block = jnp.concatenate([ag[slot, j, part(p)], ag[slot + 2, j, part(p)]], axis=1)
                acc[core, part(p), :] += dot(block, weight, NT)

    def span(group):
        return pl.ds(group * GROUP, GROUP)

    def stage_mid(group):
        @pl.loop(group * GROUP, group * GROUP + GROUP)
        def _(unit):
            landed(yrecv.at[unit, 0], y1_sem.at[unit])
            for to, p, slot, k in ((up, 0, 1, 1), (down, 1, 2, 3)):
                total = ysend[unit, to, quads(p)].astype(F32)
                total += yrecv[unit, 0, quads(p)].astype(F32)
                ysend[unit, to, quads(p)] = total.astype(BF16)
                send_y(unit, to, p, slot, y_sem, k)

    def stage_y(group):
        @pl.loop(group * GROUP, group * GROUP + GROUP)
        def _(unit):
            landed(yrecv.at[unit, pl.ds(1, 2)], y_sem.at[unit])
            total = ysend[unit, y].astype(F32)
            for k in (1, 2):
                total += yrecv[unit, k].astype(F32)
            z0[:, unit] = total.astype(BF16)

        remote(
            z0.at[pl.ds(4 - 4 * bits[0], 4), span(group)], r0.at[:, span(group)],
            send_sem.at[4], z_sem.at[0, group], half_peer(0),
        ).start()

    def stage_0(group):
        landed(r0.at[:, span(group)], z_sem.at[0, group])
        kept = z0[pl.ds(4 * bits[0], 4), span(group)].astype(F32)
        z1[:, span(group)] = (kept + r0[:, span(group)].astype(F32)).astype(BF16)
        remote(
            z1.at[pl.ds(2 - 2 * bits[1], 2), span(group)], r1.at[:, span(group)],
            send_sem.at[5], z_sem.at[1, group], half_peer(1),
        ).start()

    def stage_1(group):
        landed(r1.at[:, span(group)], z_sem.at[1, group])
        kept = z1[pl.ds(2 * bits[1], 2), span(group)].astype(F32)
        z2[:, span(group)] = (kept + r1[:, span(group)].astype(F32)).astype(BF16)
        remote(
            z2.at[1 - bits[2], span(group)], r2.at[span(group)],
            send_sem.at[6], z_sem.at[2, group], half_peer(2),
        ).start()

    def stage_2(group):
        landed(r2.at[span(group)], z_sem.at[2, group])

        @pl.loop(group * GROUP, group * GROUP + GROUP)
        def _(unit):
            total = z2[bits[2], unit].astype(F32) + r2[unit].astype(F32)
            total = total.astype(BF16)
            mine = jnp.where(c == 0, total[:, :8], total[:, 8:])
            other = jnp.where(c == 0, total[:, 8:], total[:, :8])
            slot, owners, j = place(unit)
            for k in range(2):
                wgrad_ref[:, pl.ds(column(owners[k], c, j), LANES)] = mine[k]
            wsend[unit] = other.reshape(ROWS, LANES)

    def swap(which, first, count):
        rows = pl.ds(first, count)
        remote(
            wsend.at[rows], wrecv.at[rows], send_sem.at[13], out_sem.at[which], core_peer
        ).start()

    def arrive_swap(which, first, count):
        rows = pl.ds(first, count)
        landed(wrecv.at[rows], out_sem.at[which])

        @pl.loop(first, first + count)
        def _(unit):
            slot, owners, j = place(unit)
            for k in range(2):
                wgrad_ref[:, pl.ds(column(owners[k], 1 - c, j), LANES)] = wrecv[
                    unit, k * 8:(k + 1) * 8
                ]

    def when(condition, work, *args):
        @pl.when(condition)
        def _():
            work(*args)

    EARLY = [
        (0, arrive_near, 0), (0, arrive_near, 1), (0, pass_on, 0), (0, arrive_near, 2),
        (0, arrive_weights), (1, pass_on, 1),
    ]
    LATE = [
        (2, arrive_far, 0), (2, pass_on, 2), (2, stage_mid, 0), (2, stage_mid, 1), (2, stage_mid, 2),
        (2, arrive_near, 3), (2, arrive_far, 1), (2, stage_y, 0), (2, stage_y, 1),
        (3, arrive_far, 2), (3, arrive_near, 4), (3, stage_y, 2), (3, stage_0, 0),
        (4, arrive_near, 5), (4, stage_0, 1), (4, stage_0, 2), (4, stage_mid, 3), (4, stage_1, 0),
        (4, stage_mid, 4),
    ]

    @pl.loop(0, GROUPS)
    def _(group):
        for at, work, *args in EARLY:
            when(group == at, work, *args)

        @pl.loop(group * GROUP, group * GROUP + GROUP)
        def _(unit):
            when(lax.rem(unit, GROUP) == 1, arrive_opposite, group)
            project(unit)

        for at, work, *args in LATE:
            when(group == at, work, *args)

    gains = [[None, None], [None, None]]

    def backward(image, head):
        pair = image * 2 + head
        rows = pl.ds(image * PATCHES, PATCHES)
        cols = pl.ds(head * HEAD, HEAD)
        grad = (acc[c, rows, cols] + accr[rows, cols]).astype(BF16)
        weights = probs[pair]
        vgrad_ref[rows, cols] = dot(weights.astype(BF16), grad).astype(BF16)
        upstream = dot(v[rows, cols], grad, NT)
        row_dot = jnp.sum(weights * upstream, axis=0, keepdims=True)
        score = (weights * (upstream - row_dot) * factor).astype(BF16)
        kup = dot(score, qu[pair])
        qup = dot(score, ku[pair], TN)
        for which, (up, normed, inverse, gain, out) in enumerate((
            (qup, qn[pair], qinv[pair], qg_ref[pl.ds(head, 1), :], qgrad_ref),
            (kup, kn[pair], kinv[pair], kg_ref[pl.ds(head, 1), :], kgrad_ref),
        )):
            term = jnp.sum(up * normed, axis=0, keepdims=True)
            old = gains[which][head]
            gains[which][head] = term if old is None else old + term
            out[rows, cols] = norm_backward(up, normed, inverse, gain).astype(BF16)

    for image in range(2):
        remote(
            acc.at[1 - c, part(image)], accr.at[part(image)],
            send_sem.at[12], acc_sem.at[image], core_peer,
        ).start()
    stage_y(3)
    stage_1(1)
    stage_1(2)
    stage_mid(5)
    for image in range(2):
        landed(accr.at[part(image)], acc_sem.at[image])
        for head in range(2):
            backward(image, head)

    gown[...] = jnp.zeros_like(gown)
    for which in range(2):
        for head in range(2):
            gown[pl.ds(which * 2 + head, 1), :] = gains[which][head] * (1.0 / 32.0)
    for k in (1, 3, 2):
        remote(gown, gy.at[k - 1], send_sem.at[7], gy_sem, y_peer(k)).start()

    def gain_pair(stage):
        remote(
            gsum.at[stage], gz.at[stage], send_sem.at[8 + stage], gz_sem.at[stage],
            half_peer(stage),
        ).start()

    stage_y(4)
    stage_y(5)
    stage_0(3)
    stage_0(4)
    for group in range(3):
        stage_2(group)
    landed(gy, gy_sem)
    gsum[0] = gown[...] + gy[0] + gy[1] + gy[2]
    gain_pair(0)
    stage_0(5)
    stage_1(3)
    stage_1(4)
    landed(gz.at[0], gz_sem.at[0])
    gsum[1] = gsum[0] + gz[0]
    gain_pair(1)
    stage_1(5)
    landed(gz.at[1], gz_sem.at[1])
    gsum[2] = gsum[1] + gz[1]
    gain_pair(2)
    stage_2(3)
    stage_2(4)
    swap(0, 0, 5 * GROUP)
    stage_2(5)
    swap(1, 5 * GROUP, GROUP)
    arrive_swap(0, 0, 5 * GROUP)
    landed(gz.at[2], gz_sem.at[2])
    total = gsum[2] + gz[2]
    qgg_ref[...] = total[0:2]
    kgg_ref[...] = total[2:4]

    arrive_swap(1, 5 * GROUP, GROUP)

    landed(ag.at[pl.ds(0, 2)], send_sem.at[0])
    landed(ag.at[pl.ds(0, 6)], send_sem.at[1])
    landed(w2.at[0], send_sem.at[2])
    landed(att.at[0], send_sem.at[11])
    landed(accr, send_sem.at[12])
    landed(wrecv, send_sem.at[13])
    landed(yrecv, send_sem.at[3])
    landed(r0, send_sem.at[4])
    landed(r1, send_sem.at[5])
    landed(r2, send_sem.at[6])
    landed(gy, send_sem.at[7])
    for stage in range(3):
        landed(gz.at[stage], send_sem.at[8 + stage])


def place_outputs(*refs):
    for source, target in zip(refs[:6], refs[6:]):
        target[...] = source[...]


def local(cotangent, out_weight, query_raw, key_raw, value, query_gain, key_gain):
    anywhere = pl.BlockSpec(memory_space=pl.ANY)
    vmem = pl.BlockSpec(memory_space=pltpu.VMEM)
    pair = (4, PATCHES, HEAD)
    outs = pl.pallas_call(
        kernel,
        out_shape=(
            jax.ShapeDtypeStruct((TOK, 256), BF16),
            jax.ShapeDtypeStruct((TOK, 256), BF16),
            jax.ShapeDtypeStruct((TOK, 256), BF16),
            jax.ShapeDtypeStruct((8, 6144), BF16),
            jax.ShapeDtypeStruct((2, HEAD), F32),
            jax.ShapeDtypeStruct((2, HEAD), F32),
        ),
        in_specs=[anywhere] * 5 + [vmem] * 2,
        out_specs=[vmem] * 6,
        scratch_shapes=[
            pltpu.VMEM((CHIPS, BLOCKS, TOK, LANES), BF16),
            pltpu.VMEM((BLOCKS, 2, 256, LANES), BF16),
            pltpu.VMEM((2, CHIPS, 256, 384), BF16),
            pltpu.VMEM((TOK, 256), BF16),
            pltpu.VMEM((TOK, 256), BF16),
            pltpu.VMEM((TOK, 256), BF16),
            pltpu.VMEM(pair, F32),
            pltpu.VMEM(pair, F32),
            pltpu.VMEM((4, PATCHES, 1), F32),
            pltpu.VMEM((4, PATCHES, 1), F32),
            pltpu.VMEM(pair, BF16),
            pltpu.VMEM(pair, BF16),
            pltpu.VMEM((4, PATCHES, PATCHES), F32),
            pltpu.VMEM((2, 256, TOK), BF16),
            pltpu.VMEM((2, TOK, 256), F32),
            pltpu.VMEM((TOK, 256), F32),
            pltpu.VMEM((UNITS, NY, NZ, 2, ROWS, LANES), BF16),
            pltpu.VMEM((UNITS, NY - 1, NZ, 2, ROWS, LANES), BF16),
            pltpu.VMEM((NZ, UNITS, 2, ROWS, LANES), BF16),
            pltpu.VMEM((4, UNITS, 2, ROWS, LANES), BF16),
            pltpu.VMEM((4, UNITS, 2, ROWS, LANES), BF16),
            pltpu.VMEM((2, UNITS, 2, ROWS, LANES), BF16),
            pltpu.VMEM((2, UNITS, 2, ROWS, LANES), BF16),
            pltpu.VMEM((UNITS, 2, ROWS, LANES), BF16),
            pltpu.VMEM((UNITS, ROWS, LANES), BF16),
            pltpu.VMEM((UNITS, ROWS, LANES), BF16),
            pltpu.VMEM((8, LANES), F32),
            pltpu.VMEM((NY - 1, 8, LANES), F32),
            pltpu.VMEM((3, 8, LANES), F32),
            pltpu.VMEM((3, 8, LANES), F32),
            pltpu.SemaphoreType.DMA((4 + BLOCKS,)),
            pltpu.SemaphoreType.DMA((14,)),
            pltpu.SemaphoreType.DMA((BLOCKS, 2)),
            pltpu.SemaphoreType.DMA((BLOCKS, 2)),
            pltpu.SemaphoreType.DMA((CHIPS, BLOCKS)),
            pltpu.SemaphoreType.DMA((2,)),
            pltpu.SemaphoreType.DMA((2,)),
            pltpu.SemaphoreType.DMA((2,)),
            pltpu.SemaphoreType.DMA((UNITS,)),
            pltpu.SemaphoreType.DMA((UNITS,)),
            pltpu.SemaphoreType.DMA((3, GROUPS)),
            pltpu.SemaphoreType.DMA,
            pltpu.SemaphoreType.DMA((3,)),
        ],
        compiler_params=pltpu.CompilerParams(
            collective_id=0, has_side_effects=True, vmem_limit_bytes=60 << 20
        ),
        cost_estimate=pl.CostEstimate(
            flops=4 * 10**9, bytes_accessed=6 * 10**6, transcendentals=4 * 65536
        ),
        name="attention_backward",
    )(cotangent, out_weight, query_raw, key_raw, value, query_gain, key_gain)
    return pl.pallas_call(
        place_outputs,
        out_shape=tuple(jax.ShapeDtypeStruct(out.shape, out.dtype) for out in outs),
        in_specs=[vmem] * 6,
        out_specs=[vmem] * 6,
        compiler_params=pltpu.CompilerParams(vmem_limit_bytes=60 << 20),
        name="place_outputs",
    )(*outs)


def solution(mesh):
    return jax.shard_map(
        local,
        mesh=mesh,
        in_specs=(
            P("dp", "mp"),
            P("mp", None),
            P("dp", "mp"),
            P("dp", "mp"),
            P("dp", "mp"),
            P("mp", None),
            P("mp", None),
        ),
        out_specs=(
            P("dp", "mp"),
            P("dp", "mp"),
            P("dp", "mp"),
            P(("mp", "dp"), None),
            P("mp", None),
            P("mp", None),
        ),
        check_vma=False,
    )
```

```python
import jax
import jax.numpy as jnp
from jax import lax
from jax.experimental import pallas as pl
from jax.experimental.pallas import tpu as pltpu
from jax.sharding import PartitionSpec as P

MESH = pl.DeviceIdType.MESH
F32 = jnp.float32
BF16 = jnp.bfloat16

PATCHES = 256
HEAD = 128
EPSILON = 1e-06
TOK = 512
LANES = 128
CHIPS = 8
BLOCKS = 3
UNITS = CHIPS * BLOCKS // 2
GROUP = 2
GROUPS = UNITS // GROUP
NY = 4
NZ = 8
ROWS = 16
REVERSED = (0, 4, 2, 6, 1, 5, 3, 7)

NT = (((1,), (1,)), ((), ()))
TN = (((0,), (0,)), ((), ()))


def dot(a, b, dims=(((1,), (0,)), ((), ()))):
    return lax.dot_general(a, b, dims, preferred_element_type=F32)


def normalize(raw):
    floats = raw.astype(F32)
    center = floats - jnp.mean(floats, axis=-1, keepdims=True)
    inverse = lax.rsqrt(jnp.mean(center * center, axis=-1, keepdims=True) + EPSILON)
    return center * inverse, inverse


def norm_backward(upstream, normed, inverse, gain):
    scaled = upstream * gain
    centered = scaled - jnp.mean(scaled, axis=-1, keepdims=True)
    return inverse * (centered - normed * jnp.mean(scaled * normed, axis=-1, keepdims=True))


def kernel(
    cot_hbm, w_hbm, q_hbm, k_hbm, v_hbm, qg_ref, kg_ref,
    qgrad_ref, kgrad_ref, vgrad_ref, wgrad_ref, qgg_ref, kgg_ref,
    ag, transit, w2, qraw, kraw, v, qn, kn, qinv, kinv, qu, ku, probs, att, acc, accr,
    ysend, yrecv, z0, r0, z2, r2, gown, gy, gsum, gz,
    local_sem, send_sem, leg_sem, far_sem, x_sem, core_sem, acc_sem, y1_sem, y_sem, z_sem, gy_sem, gz_sem,
):
    d = lax.axis_index("dp")
    m = lax.axis_index("mp")
    y = lax.rem(d, NY)
    zl = d // NY
    x = m // 4
    zh = lax.rem(m // 2, 2)
    c = lax.rem(m, 2)
    z = zh * NZ + zl
    bits = [lax.rem(zl // step, 2) for step in (1, 2, 4)]

    def x_peer(k):
        return (d, lax.rem(x + k, 4) * 4 + zh * 2 + c)

    def y_peer(k):
        return (zl * NY + lax.rem(y + k, NY), m)

    def z_peer(k):
        other = lax.rem(z + k, 2 * NZ)
        return (lax.rem(other, NZ) * NY + y, x * 4 + (other // NZ) * 2 + c)

    def flip(stage):
        step = 1 << stage
        return step - 2 * step * bits[stage]

    def quad_peer(k):
        return ((zl + flip(0) * (k // 2) + flip(1) * (k % 2)) * NY + y, m)

    half_peer = ((zl + flip(2)) * NY + y, m)
    half_cross = ((zl + flip(2)) * NY + y, m + 1 - 2 * c)
    quad = bits[0] * 2 + bits[1]

    core_peer = (d, m + 1 - 2 * c)

    barrier = pltpu.get_barrier_semaphore()
    peers = [z_peer(4), z_peer(12), core_peer, half_cross]
    peers += [quad_peer(k) for k in (1, 2, 3)]
    peers += [x_peer(k) for k in (1, 3)]
    peers += [y_peer(k) for k in (1, 2, 3)]
    for peer in peers:
        pl.semaphore_signal(barrier, inc=1, device_id=peer, device_id_type=MESH)

    loads = [
        pltpu.make_async_copy(q_hbm, qraw, local_sem.at[0]),
        pltpu.make_async_copy(k_hbm, kraw, local_sem.at[1]),
        pltpu.make_async_copy(v_hbm, v, local_sem.at[2]),
    ]
    for j in range(BLOCKS):
        loads.append(
            pltpu.make_async_copy(
                cot_hbm.at[:, pl.ds(j * LANES, LANES)], ag.at[0, j], local_sem.at[3 + j]
            )
        )
    for chip in range(CHIPS):
        start = pl.multiple_of(chip * 768 + c * 384, LANES)
        loads.append(
            pltpu.make_async_copy(
                w_hbm.at[:, pl.ds(start, 384)], w2.at[c, chip], local_sem.at[3 + BLOCKS]
            )
        )
    for load in loads:
        load.start()

    def remote(src, dst, sent, landed, peer):
        return pltpu.make_async_remote_copy(
            src_ref=src, dst_ref=dst, send_sem=sent, recv_sem=landed,
            device_id=peer, device_id_type=MESH,
        )

    def landed(ref, sem):
        pltpu.make_async_copy(ref, ref, sem).wait()

    def send_x(slot, j):
        for k in (1, 3):
            remote(
                ag.at[slot, j], ag.at[slot + 4 - k, j],
                send_sem.at[1], x_sem.at[slot + 4 - k, j], x_peer(k),
            ).start()

    def part(p):
        return pl.ds(p * 256, 256)

    factor = HEAD ** (-0.5)

    def forward(image, head):
        pair = image * 2 + head
        rows = pl.ds(image * PATCHES, PATCHES)
        cols = pl.ds(head * HEAD, HEAD)
        normed, inverse = normalize(qraw[rows, cols])
        qn[pair] = normed
        qinv[pair] = inverse
        query = (normed * qg_ref[pl.ds(head, 1), :]).astype(BF16)
        qu[pair] = query
        normed, inverse = normalize(kraw[rows, cols])
        kn[pair] = normed
        kinv[pair] = inverse
        keys = (normed * kg_ref[pl.ds(head, 1), :]).astype(BF16)
        ku[pair] = keys
        scores = dot(keys, query, NT) * factor
        weights = jnp.exp(scores - jnp.max(scores, axis=0, keepdims=True))
        weights = weights / jnp.sum(weights, axis=0, keepdims=True)
        probs[pair] = weights
        attended = dot(v[rows, cols], weights.astype(BF16), TN)
        att[c, cols, rows] = attended.astype(BF16)

    pl.semaphore_wait(barrier, len(peers))
    def send_leg(j):
        for p in range(2):
            remote(
                cot_hbm.at[part(p), pl.ds(j * LANES, LANES)], transit.at[j, p],
                send_sem.at[0], leg_sem.at[j, p], z_peer(4 + 8 * p),
            ).start()

    send_leg(0)
    send_leg(1)
    for load in loads[3:3 + BLOCKS]:
        load.wait()
    for j in range(BLOCKS):
        send_x(0, j)
    for chip in range(CHIPS):
        start = pl.multiple_of(chip * 768 + (1 - c) * 384, LANES)
        remote(
            w_hbm.at[:, pl.ds(start, 384)], w2.at[c, chip],
            send_sem.at[2], core_sem.at[0], core_peer,
        ).start()
    for load in loads[:3]:
        load.wait()
    for image in range(2):
        for head in range(2):
            forward(image, head)
    remote(att.at[c], att.at[c], send_sem.at[11], core_sem.at[1], core_peer).start()
    acc[...] = jnp.zeros_like(acc)
    landed(w2.at[c], local_sem.at[3 + BLOCKS])

    def arrive_weights():
        landed(w2.at[1 - c], core_sem.at[0])
        landed(att.at[1 - c], core_sem.at[1])

    def pass_on(j):
        for p in range(2):
            landed(transit.at[j, p], leg_sem.at[j, p])
            remote(
                transit.at[j, p], ag.at[4, j, part(p)],
                send_sem.at[0], far_sem.at[j, p], z_peer(4 + 8 * p),
            ).start()
        if j == 0:
            send_leg(2)

    def arrive_far(j):
        for p in range(2):
            landed(ag.at[4, j, part(p)], far_sem.at[j, p])
        send_x(4, j)

    def arrive_near(group):
        half, j = divmod(group, BLOCKS)
        for k, p in ((1, 1), (3, 0)):
            slot = half * 4 + k
            landed(ag.at[slot, j], x_sem.at[slot, j])
            remote(
                ag.at[slot, j, part(p)], ag.at[half * 4 + 2, j, part(p)],
                send_sem.at[1], x_sem.at[half * 4 + 2, j], x_peer(4 - k),
            ).start()

    def arrive_opposite(group):
        slot = (group // BLOCKS) * 4 + 2
        j = lax.rem(group, BLOCKS)
        landed(ag.at[slot, j], x_sem.at[slot, j])

    def place(unit):
        group = unit // GROUP
        half = group // BLOCKS
        near = 1 - lax.rem(unit, GROUP)
        owners = [
            lax.rem(x + near + k, 4) * 2 + lax.rem(zh + half, 2) for k in (0, 2)
        ]
        return half * 4 + near, owners, lax.rem(group, BLOCKS)

    def column(owner, core, j):
        return pl.multiple_of(owner * 768 + core * 384 + j * LANES, LANES)

    up, across, down = [lax.rem(y + k, NY) for k in (1, 2, 3)]

    def quads(p):
        return pl.ds(p * 4, 4)

    def send_y(unit, to, p, slot, sem, k):
        remote(
            ysend.at[unit, to, quads(p)], yrecv.at[unit, slot, quads(p)],
            send_sem.at[3], sem.at[unit], y_peer(k),
        ).start()

    def project(unit):
        slot, owners, j = place(unit)
        cols = pl.ds(pl.multiple_of(j * LANES, LANES), LANES)
        block = jnp.concatenate([ag[slot, j], ag[slot + 2, j]], axis=1)
        for core in range(2):
            terms = (dot(att[core], block) * (1.0 / 32.0)).reshape(NZ, NY, 8, 2 * LANES)
            both = jnp.concatenate([terms[..., :LANES], terms[..., LANES:]], axis=2).astype(BF16)
            for to in range(NZ):
                for p in range(NY):
                    ysend[unit, p, REVERSED[to], core] = both[to, p]
        send_y(unit, across, 0, 0, y1_sem, 1)
        send_y(unit, across, 1, 0, y1_sem, 3)
        send_y(unit, up, 1, 1, y_sem, 1)
        send_y(unit, down, 0, 2, y_sem, 3)
        for core in range(2):
            weight = jnp.concatenate([w2[core, owner, :, cols] for owner in owners], axis=1)
            for p in range(2):
                block = jnp.concatenate([ag[slot, j, part(p)], ag[slot + 2, j, part(p)]], axis=1)
                acc[core, part(p), :] += dot(block, weight, NT)

    def span(group):
        return pl.ds(group * GROUP, GROUP)

    def stage_mid(group):
        @pl.loop(group * GROUP, group * GROUP + GROUP)
        def _(unit):
            landed(yrecv.at[unit, 0], y1_sem.at[unit])
            for to, p, slot, k in ((up, 0, 1, 1), (down, 1, 2, 3)):
                total = ysend[unit, to, quads(p)].astype(F32)
                total += yrecv[unit, 0, quads(p)].astype(F32)
                ysend[unit, to, quads(p)] = total.astype(BF16)
                send_y(unit, to, p, slot, y_sem, k)

    def stage_y(group):
        @pl.loop(group * GROUP, group * GROUP + GROUP)
        def _(unit):
            landed(yrecv.at[unit, pl.ds(1, 2)], y_sem.at[unit])
            total = ysend[unit, y].astype(F32)
            for k in (1, 2):
                total += yrecv[unit, k].astype(F32)
            z0[:, unit] = total.astype(BF16)

        for k in (1, 2, 3):
            other = lax.rem(bits[0] + k // 2, 2) * 2 + lax.rem(bits[1] + k % 2, 2)
            remote(
                z0.at[pl.ds(2 * other, 2), span(group)], r0.at[k - 1, :, span(group)],
                send_sem.at[4], z_sem.at[0, group], quad_peer(k),
            ).start()

    def stage_0(group):
        landed(r0.at[:, :, span(group)], z_sem.at[0, group])
        total = z0[pl.ds(2 * quad, 2), span(group)].astype(F32)
        for k in range(3):
            total += r0[k, :, span(group)].astype(F32)
        z2[:, span(group)] = total.astype(BF16)
        for source, slot, peer in (
            (z2.at[1 - bits[2], span(group), c], 0, half_peer),
            (z2.at[1 - bits[2], span(group), 1 - c], 1, half_cross),
            (z2.at[bits[2], span(group), 1 - c], 2, core_peer),
        ):
            remote(
                source, r2.at[slot, span(group)], send_sem.at[5], z_sem.at[1, group], peer
            ).start()

    def stage_2(group):
        landed(r2.at[:, span(group)], z_sem.at[1, group])

        @pl.loop(group * GROUP, group * GROUP + GROUP)
        def _(unit):
            slot, owners, j = place(unit)
            mine = (z2[bits[2], unit, c].astype(F32) + r2[0, unit].astype(F32)).astype(BF16)
            other = (r2[1, unit].astype(F32) + r2[2, unit].astype(F32)).astype(BF16)
            for k in range(2):
                rows = slice(k * 8, k * 8 + 8)
                wgrad_ref[:, pl.ds(column(owners[k], c, j), LANES)] = mine[rows]
                wgrad_ref[:, pl.ds(column(owners[k], 1 - c, j), LANES)] = other[rows]

    def when(condition, work, *args):
        @pl.when(condition)
        def _():
            work(*args)

    EARLY = [
        (0, arrive_near, 0), (0, arrive_near, 1), (0, pass_on, 0), (0, arrive_near, 2),
        (0, arrive_weights), (1, pass_on, 1),
    ]
    LATE = [
        (2, arrive_far, 0), (2, pass_on, 2), (2, stage_mid, 0), (2, stage_mid, 1), (2, stage_mid, 2),
        (2, arrive_near, 3), (2, arrive_far, 1), (2, stage_y, 0), (2, stage_y, 1),
        (3, arrive_far, 2), (3, arrive_near, 4), (3, stage_y, 2),
        (4, stage_mid, 3), (4, arrive_near, 5), (4, stage_0, 0), (4, stage_0, 1), (4, stage_0, 2),
    ]

    @pl.loop(0, GROUPS)
    def _(group):
        for at, work, *args in EARLY:
            when(group == at, work, *args)

        @pl.loop(group * GROUP, group * GROUP + GROUP)
        def _(unit):
            when(unit == UNITS - 1, stage_mid, GROUPS - 2)
            when(lax.rem(unit, GROUP) == 1, arrive_opposite, group)
            project(unit)

        for at, work, *args in LATE:
            when(group == at, work, *args)

    gains = [[None, None], [None, None]]

    def backward(image, head):
        pair = image * 2 + head
        rows = pl.ds(image * PATCHES, PATCHES)
        cols = pl.ds(head * HEAD, HEAD)
        grad = (acc[c, rows, cols] + accr[rows, cols]).astype(BF16)
        weights = probs[pair]
        vgrad_ref[rows, cols] = dot(weights.astype(BF16), grad).astype(BF16)
        upstream = dot(v[rows, cols], grad, NT)
        row_dot = jnp.sum(weights * upstream, axis=0, keepdims=True)
        score = (weights * (upstream - row_dot) * factor).astype(BF16)
        kup = dot(score, qu[pair])
        qup = dot(score, ku[pair], TN)
        for which, (up, normed, inverse, gain, out) in enumerate((
            (qup, qn[pair], qinv[pair], qg_ref[pl.ds(head, 1), :], qgrad_ref),
            (kup, kn[pair], kinv[pair], kg_ref[pl.ds(head, 1), :], kgrad_ref),
        )):
            term = jnp.sum(up * normed, axis=0, keepdims=True)
            old = gains[which][head]
            gains[which][head] = term if old is None else old + term
            out[rows, cols] = norm_backward(up, normed, inverse, gain).astype(BF16)

    for image in range(2):
        remote(
            acc.at[1 - c, part(image)], accr.at[part(image)],
            send_sem.at[12], acc_sem.at[image], core_peer,
        ).start()
    stage_y(3)
    stage_2(0)
    stage_mid(5)
    for image in range(2):
        landed(accr.at[part(image)], acc_sem.at[image])
        for head in range(2):
            backward(image, head)

    gown[...] = jnp.zeros_like(gown)
    for which in range(2):
        for head in range(2):
            gown[pl.ds(which * 2 + head, 1), :] = gains[which][head] * (1.0 / 32.0)
    for k in (1, 3, 2):
        remote(gown, gy.at[k - 1], send_sem.at[7], gy_sem, y_peer(k)).start()

    stage_y(4)
    stage_y(5)
    stage_0(3)
    landed(gy, gy_sem)
    gsum[0] = gown[...] + gy[0] + gy[1] + gy[2]
    for k in (1, 2, 3):
        remote(
            gsum.at[0], gz.at[k - 1], send_sem.at[6], gz_sem.at[0], quad_peer(k)
        ).start()
    stage_0(4)
    stage_2(1)
    stage_2(2)
    stage_0(5)
    landed(gz.at[pl.ds(0, 3)], gz_sem.at[0])
    gsum[1] = gsum[0] + gz[0] + gz[1] + gz[2]
    remote(gsum.at[1], gz.at[3], send_sem.at[8], gz_sem.at[1], half_peer).start()
    stage_2(3)
    stage_2(4)
    stage_2(5)
    landed(gz.at[3], gz_sem.at[1])
    total = gsum[1] + gz[3]
    qgg_ref[...] = total[0:2]
    kgg_ref[...] = total[2:4]

    landed(ag.at[pl.ds(0, 2)], send_sem.at[0])
    landed(ag.at[pl.ds(0, 6)], send_sem.at[1])
    landed(w2.at[0], send_sem.at[2])
    landed(att.at[0], send_sem.at[11])
    landed(accr, send_sem.at[12])
    landed(yrecv, send_sem.at[3])
    landed(r0, send_sem.at[4])
    landed(r2, send_sem.at[5])
    landed(gz.at[pl.ds(0, 3)], send_sem.at[6])
    landed(gy, send_sem.at[7])
    landed(gz.at[3], send_sem.at[8])


def place_outputs(*refs):
    for source, target in zip(refs[:6], refs[6:]):
        target[...] = source[...]


def local(cotangent, out_weight, query_raw, key_raw, value, query_gain, key_gain):
    anywhere = pl.BlockSpec(memory_space=pl.ANY)
    vmem = pl.BlockSpec(memory_space=pltpu.VMEM)
    pair = (4, PATCHES, HEAD)
    outs = pl.pallas_call(
        kernel,
        out_shape=(
            jax.ShapeDtypeStruct((TOK, 256), BF16),
            jax.ShapeDtypeStruct((TOK, 256), BF16),
            jax.ShapeDtypeStruct((TOK, 256), BF16),
            jax.ShapeDtypeStruct((8, 6144), BF16),
            jax.ShapeDtypeStruct((2, HEAD), F32),
            jax.ShapeDtypeStruct((2, HEAD), F32),
        ),
        in_specs=[anywhere] * 5 + [vmem] * 2,
        out_specs=[vmem] * 6,
        scratch_shapes=[
            pltpu.VMEM((CHIPS, BLOCKS, TOK, LANES), BF16),
            pltpu.VMEM((BLOCKS, 2, 256, LANES), BF16),
            pltpu.VMEM((2, CHIPS, 256, 384), BF16),
            pltpu.VMEM((TOK, 256), BF16),
            pltpu.VMEM((TOK, 256), BF16),
            pltpu.VMEM((TOK, 256), BF16),
            pltpu.VMEM(pair, F32),
            pltpu.VMEM(pair, F32),
            pltpu.VMEM((4, PATCHES, 1), F32),
            pltpu.VMEM((4, PATCHES, 1), F32),
            pltpu.VMEM(pair, BF16),
            pltpu.VMEM(pair, BF16),
            pltpu.VMEM((4, PATCHES, PATCHES), F32),
            pltpu.VMEM((2, 256, TOK), BF16),
            pltpu.VMEM((2, TOK, 256), F32),
            pltpu.VMEM((TOK, 256), F32),
            pltpu.VMEM((UNITS, NY, NZ, 2, ROWS, LANES), BF16),
            pltpu.VMEM((UNITS, NY - 1, NZ, 2, ROWS, LANES), BF16),
            pltpu.VMEM((NZ, UNITS, 2, ROWS, LANES), BF16),
            pltpu.VMEM((3, 2, UNITS, 2, ROWS, LANES), BF16),
            pltpu.VMEM((2, UNITS, 2, ROWS, LANES), BF16),
            pltpu.VMEM((3, UNITS, ROWS, LANES), BF16),
            pltpu.VMEM((8, LANES), F32),
            pltpu.VMEM((NY - 1, 8, LANES), F32),
            pltpu.VMEM((2, 8, LANES), F32),
            pltpu.VMEM((4, 8, LANES), F32),
            pltpu.SemaphoreType.DMA((4 + BLOCKS,)),
            pltpu.SemaphoreType.DMA((13,)),
            pltpu.SemaphoreType.DMA((BLOCKS, 2)),
            pltpu.SemaphoreType.DMA((BLOCKS, 2)),
            pltpu.SemaphoreType.DMA((CHIPS, BLOCKS)),
            pltpu.SemaphoreType.DMA((2,)),
            pltpu.SemaphoreType.DMA((2,)),
            pltpu.SemaphoreType.DMA((UNITS,)),
            pltpu.SemaphoreType.DMA((UNITS,)),
            pltpu.SemaphoreType.DMA((2, GROUPS)),
            pltpu.SemaphoreType.DMA,
            pltpu.SemaphoreType.DMA((2,)),
        ],
        compiler_params=pltpu.CompilerParams(
            collective_id=0, has_side_effects=True, vmem_limit_bytes=60 << 20
        ),
        cost_estimate=pl.CostEstimate(
            flops=4 * 10**9, bytes_accessed=6 * 10**6, transcendentals=4 * 65536
        ),
        name="attention_backward",
    )(cotangent, out_weight, query_raw, key_raw, value, query_gain, key_gain)
    return pl.pallas_call(
        place_outputs,
        out_shape=tuple(jax.ShapeDtypeStruct(out.shape, out.dtype) for out in outs),
        in_specs=[vmem] * 6,
        out_specs=[vmem] * 6,
        compiler_params=pltpu.CompilerParams(vmem_limit_bytes=60 << 20),
        name="place_outputs",
    )(*outs)


def solution(mesh):
    return jax.shard_map(
        local,
        mesh=mesh,
        in_specs=(
            P("dp", "mp"),
            P("mp", None),
            P("dp", "mp"),
            P("dp", "mp"),
            P("dp", "mp"),
            P("mp", None),
            P("mp", None),
        ),
        out_specs=(
            P("dp", "mp"),
            P("dp", "mp"),
            P("dp", "mp"),
            P(("mp", "dp"), None),
            P("mp", None),
            P("mp", None),
        ),
        check_vma=False,
    )
```

```python
import jax
import jax.numpy as jnp
from jax import lax
from jax.experimental import pallas as pl
from jax.experimental.pallas import tpu as pltpu
from jax.sharding import PartitionSpec as P

MESH = pl.DeviceIdType.MESH
F32 = jnp.float32
BF16 = jnp.bfloat16

PATCHES = 256
HEAD = 128
EPSILON = 1e-06
TOK = 512
LANES = 128
CHIPS = 8
BLOCKS = 3
UNITS = CHIPS * BLOCKS // 2
GROUP = 2
GROUPS = UNITS // GROUP
NY = 4
NZ = 8
ROWS = 16
REVERSED = (0, 4, 2, 6, 1, 5, 3, 7)

NT = (((1,), (1,)), ((), ()))
TN = (((0,), (0,)), ((), ()))


def dot(a, b, dims=(((1,), (0,)), ((), ()))):
    return lax.dot_general(a, b, dims, preferred_element_type=F32)


def normalize(raw):
    floats = raw.astype(F32)
    center = floats - jnp.mean(floats, axis=-1, keepdims=True)
    inverse = lax.rsqrt(jnp.mean(center * center, axis=-1, keepdims=True) + EPSILON)
    return center * inverse, inverse


def norm_backward(upstream, normed, inverse, gain):
    scaled = upstream * gain
    centered = scaled - jnp.mean(scaled, axis=-1, keepdims=True)
    return inverse * (centered - normed * jnp.mean(scaled * normed, axis=-1, keepdims=True))


def kernel(
    cot_hbm, w_hbm, q_hbm, k_hbm, v_hbm, qg_ref, kg_ref,
    qgrad_ref, kgrad_ref, vgrad_ref, wgrad_ref, qgg_ref, kgg_ref,
    ag, transit, w2, qraw, kraw, v, qn, kn, qinv, kinv, qu, ku, probs, att, acc, accr,
    ysend, yrecv, z0, r0, z2, r2, gown, gy, gsum, gz,
    local_sem, send_sem, leg_sem, far_sem, x_sem, core_sem, acc_sem, y1_sem, y_sem, z_sem, gy_sem, gz_sem,
):
    d = lax.axis_index("dp")
    m = lax.axis_index("mp")
    y = lax.rem(d, NY)
    zl = d // NY
    x = m // 4
    zh = lax.rem(m // 2, 2)
    c = lax.rem(m, 2)
    z = zh * NZ + zl
    bits = [lax.rem(zl // step, 2) for step in (1, 2, 4)]

    def x_peer(k):
        return (d, lax.rem(x + k, 4) * 4 + zh * 2 + c)

    def y_peer(k):
        return (zl * NY + lax.rem(y + k, NY), m)

    def z_peer(k):
        other = lax.rem(z + k, 2 * NZ)
        return (lax.rem(other, NZ) * NY + y, x * 4 + (other // NZ) * 2 + c)

    def flip(stage):
        step = 1 << stage
        return step - 2 * step * bits[stage]

    def quad_peer(k):
        return ((zl + flip(0) * (k // 2) + flip(1) * (k % 2)) * NY + y, m)

    half_peer = ((zl + flip(2)) * NY + y, m)
    half_cross = ((zl + flip(2)) * NY + y, m + 1 - 2 * c)
    quad = bits[0] * 2 + bits[1]

    core_peer = (d, m + 1 - 2 * c)

    barrier = pltpu.get_barrier_semaphore()
    peers = [z_peer(4), z_peer(12), core_peer, half_cross]
    peers += [quad_peer(k) for k in (1, 2, 3)]
    peers += [x_peer(k) for k in (1, 3)]
    peers += [y_peer(k) for k in (1, 2, 3)]
    for peer in peers:
        pl.semaphore_signal(barrier, inc=1, device_id=peer, device_id_type=MESH)

    loads = [
        pltpu.make_async_copy(q_hbm, qraw, local_sem.at[0]),
        pltpu.make_async_copy(k_hbm, kraw, local_sem.at[1]),
        pltpu.make_async_copy(v_hbm, v, local_sem.at[2]),
    ]
    for j in range(BLOCKS):
        loads.append(
            pltpu.make_async_copy(
                cot_hbm.at[:, pl.ds(j * LANES, LANES)], ag.at[0, j], local_sem.at[3 + j]
            )
        )
    for chip in range(CHIPS):
        start = pl.multiple_of(chip * 768 + c * 384, LANES)
        loads.append(
            pltpu.make_async_copy(
                w_hbm.at[:, pl.ds(start, 384)], w2.at[c, chip], local_sem.at[3 + BLOCKS]
            )
        )
    for load in loads:
        load.start()

    def remote(src, dst, sent, landed, peer):
        return pltpu.make_async_remote_copy(
            src_ref=src, dst_ref=dst, send_sem=sent, recv_sem=landed,
            device_id=peer, device_id_type=MESH,
        )

    def landed(ref, sem):
        pltpu.make_async_copy(ref, ref, sem).wait()

    def send_x(slot, j):
        for k in (1, 3):
            remote(
                ag.at[slot, j], ag.at[slot + 4 - k, j],
                send_sem.at[1], x_sem.at[slot + 4 - k, j], x_peer(k),
            ).start()

    def part(p):
        return pl.ds(p * 256, 256)

    factor = HEAD ** (-0.5)

    def forward(image, head):
        pair = image * 2 + head
        rows = pl.ds(image * PATCHES, PATCHES)
        cols = pl.ds(head * HEAD, HEAD)
        normed, inverse = normalize(qraw[rows, cols])
        qn[pair] = normed
        qinv[pair] = inverse
        query = (normed * qg_ref[pl.ds(head, 1), :]).astype(BF16)
        qu[pair] = query
        normed, inverse = normalize(kraw[rows, cols])
        kn[pair] = normed
        kinv[pair] = inverse
        keys = (normed * kg_ref[pl.ds(head, 1), :]).astype(BF16)
        ku[pair] = keys
        scores = dot(keys, query, NT) * factor
        weights = jnp.exp(scores - jnp.max(scores, axis=0, keepdims=True))
        weights = weights / jnp.sum(weights, axis=0, keepdims=True)
        probs[pair] = weights
        attended = dot(v[rows, cols], weights.astype(BF16), TN)
        att[c, cols, rows] = attended.astype(BF16)

    pl.semaphore_wait(barrier, len(peers))
    def send_leg(j):
        for p in range(2):
            remote(
                cot_hbm.at[part(p), pl.ds(j * LANES, LANES)], transit.at[j, p],
                send_sem.at[0], leg_sem.at[j, p], z_peer(4 + 8 * p),
            ).start()

    send_leg(0)
    send_leg(1)
    for load in loads[3:3 + BLOCKS]:
        load.wait()
    for j in range(BLOCKS):
        send_x(0, j)
    for chip in range(CHIPS):
        start = pl.multiple_of(chip * 768 + (1 - c) * 384, LANES)
        remote(
            w_hbm.at[:, pl.ds(start, 384)], w2.at[c, chip],
            send_sem.at[2], core_sem.at[0], core_peer,
        ).start()
    for load in loads[:3]:
        load.wait()
    for image in range(2):
        for head in range(2):
            forward(image, head)
    remote(att.at[c], att.at[c], send_sem.at[11], core_sem.at[1], core_peer).start()
    acc[...] = jnp.zeros_like(acc)
    landed(w2.at[c], local_sem.at[3 + BLOCKS])

    def arrive_weights():
        landed(w2.at[1 - c], core_sem.at[0])
        landed(att.at[1 - c], core_sem.at[1])

    def pass_on(j):
        for p in range(2):
            landed(transit.at[j, p], leg_sem.at[j, p])
            remote(
                transit.at[j, p], ag.at[4, j, part(p)],
                send_sem.at[0], far_sem.at[j, p], z_peer(4 + 8 * p),
            ).start()
        if j == 0:
            send_leg(2)

    def arrive_far(j):
        for p in range(2):
            landed(ag.at[4, j, part(p)], far_sem.at[j, p])
        send_x(4, j)

    def arrive_near(group):
        half, j = divmod(group, BLOCKS)
        for k, p in ((1, 1), (3, 0)):
            slot = half * 4 + k
            landed(ag.at[slot, j], x_sem.at[slot, j])
            remote(
                ag.at[slot, j, part(p)], ag.at[half * 4 + 2, j, part(p)],
                send_sem.at[1], x_sem.at[half * 4 + 2, j], x_peer(4 - k),
            ).start()

    def arrive_opposite(group):
        slot = (group // BLOCKS) * 4 + 2
        j = lax.rem(group, BLOCKS)
        landed(ag.at[slot, j], x_sem.at[slot, j])

    def place(unit):
        group = unit // GROUP
        half = group // BLOCKS
        near = 1 - lax.rem(unit, GROUP)
        owners = [
            lax.rem(x + near + k, 4) * 2 + lax.rem(zh + half, 2) for k in (0, 2)
        ]
        return half * 4 + near, owners, lax.rem(group, BLOCKS)

    def column(owner, core, j):
        return pl.multiple_of(owner * 768 + core * 384 + j * LANES, LANES)

    up, across, down = [lax.rem(y + k, NY) for k in (1, 2, 3)]

    def quads(p):
        return pl.ds(p * 4, 4)

    def send_y(unit, to, p, slot, sem, k):
        remote(
            ysend.at[unit, to, quads(p)], yrecv.at[unit, slot, quads(p)],
            send_sem.at[3], sem.at[unit], y_peer(k),
        ).start()

    def project(unit):
        slot, owners, j = place(unit)
        cols = pl.ds(pl.multiple_of(j * LANES, LANES), LANES)
        block = jnp.concatenate([ag[slot, j], ag[slot + 2, j]], axis=1)
        for core in range(2):
            terms = (dot(att[core], block) * (1.0 / 32.0)).reshape(NZ, NY, 8, 2 * LANES)
            both = jnp.concatenate([terms[..., :LANES], terms[..., LANES:]], axis=2).astype(BF16)
            for to in range(NZ):
                for p in range(NY):
                    ysend[unit, p, REVERSED[to], core] = both[to, p]
        send_y(unit, across, 0, 0, y1_sem, 1)
        send_y(unit, across, 1, 0, y1_sem, 3)
        send_y(unit, up, 1, 1, y_sem, 1)
        send_y(unit, down, 0, 2, y_sem, 3)
        for core in range(2):
            weight = jnp.concatenate([w2[core, owner, :, cols] for owner in owners], axis=1)
            for p in range(2):
                block = jnp.concatenate([ag[slot, j, part(p)], ag[slot + 2, j, part(p)]], axis=1)
                acc[core, part(p), :] += dot(block, weight, NT)

    def stage_mid(first, count=GROUP):
        @pl.loop(first, first + count)
        def _(unit):
            landed(yrecv.at[unit, 0], y1_sem.at[unit])
            for to, p, slot, k in ((up, 0, 1, 1), (down, 1, 2, 3)):
                total = ysend[unit, to, quads(p)].astype(F32)
                total += yrecv[unit, 0, quads(p)].astype(F32)
                ysend[unit, to, quads(p)] = total.astype(BF16)
                send_y(unit, to, p, slot, y_sem, k)

    def stage_y(first, count=GROUP):
        span = pl.ds(first, count)

        @pl.loop(first, first + count)
        def _(unit):
            landed(yrecv.at[unit, pl.ds(1, 2)], y_sem.at[unit])
            total = ysend[unit, y].astype(F32)
            for k in (1, 2):
                total += yrecv[unit, k].astype(F32)
            z0[:, unit] = total.astype(BF16)

        for k in (1, 2, 3):
            other = lax.rem(bits[0] + k // 2, 2) * 2 + lax.rem(bits[1] + k % 2, 2)
            remote(
                z0.at[pl.ds(2 * other, 2), span], r0.at[k - 1, :, span],
                send_sem.at[4], z_sem.at[0, first], quad_peer(k),
            ).start()

    def stage_0(first, count=GROUP):
        span = pl.ds(first, count)
        landed(r0.at[:, :, span], z_sem.at[0, first])
        total = z0[pl.ds(2 * quad, 2), span].astype(F32)
        for k in range(3):
            total += r0[k, :, span].astype(F32)
        z2[:, span] = total.astype(BF16)
        for source, slot, peer in (
            (z2.at[1 - bits[2], span, c], 0, half_peer),
            (z2.at[1 - bits[2], span, 1 - c], 1, half_cross),
            (z2.at[bits[2], span, 1 - c], 2, core_peer),
        ):
            remote(
                source, r2.at[slot, span], send_sem.at[5], z_sem.at[1, first], peer
            ).start()

    def stage_2(first, count=GROUP):
        span = pl.ds(first, count)
        landed(r2.at[:, span], z_sem.at[1, first])

        @pl.loop(first, first + count)
        def _(unit):
            slot, owners, j = place(unit)
            mine = (z2[bits[2], unit, c].astype(F32) + r2[0, unit].astype(F32)).astype(BF16)
            other = (r2[1, unit].astype(F32) + r2[2, unit].astype(F32)).astype(BF16)
            for k in range(2):
                rows = slice(k * 8, k * 8 + 8)
                wgrad_ref[:, pl.ds(column(owners[k], c, j), LANES)] = mine[rows]
                wgrad_ref[:, pl.ds(column(owners[k], 1 - c, j), LANES)] = other[rows]

    def when(condition, work, *args):
        @pl.when(condition)
        def _():
            work(*args)

    EARLY = [
        (0, arrive_near, 0), (0, arrive_near, 1), (0, pass_on, 0), (0, arrive_near, 2),
        (0, arrive_weights), (1, pass_on, 1),
    ]
    LATE = [
        (2, arrive_far, 0), (2, pass_on, 2), (2, stage_mid, 0), (2, stage_mid, 2), (2, stage_mid, 4),
        (2, arrive_near, 3), (2, arrive_far, 1), (2, stage_y, 0), (2, stage_y, 2),
        (3, arrive_far, 2), (3, arrive_near, 4), (3, stage_y, 4),
        (4, stage_mid, 6), (4, stage_0, 0), (4, stage_0, 2), (4, stage_0, 4),
    ]

    @pl.loop(0, GROUPS)
    def _(group):
        for at, work, *args in EARLY:
            when(group == at, work, *args)

        @pl.loop(group * GROUP, group * GROUP + GROUP)
        def _(unit):
            when(unit == 9, arrive_near, 5)
            when(unit == 11, stage_mid, 8)
            when(lax.rem(unit, GROUP) == 1, arrive_opposite, group)
            project(unit)

        for at, work, *args in LATE:
            when(group == at, work, *args)

    gains = [[None, None], [None, None]]

    def backward(image, head):
        pair = image * 2 + head
        rows = pl.ds(image * PATCHES, PATCHES)
        cols = pl.ds(head * HEAD, HEAD)
        grad = (acc[c, rows, cols] + accr[rows, cols]).astype(BF16)
        weights = probs[pair]
        vgrad_ref[rows, cols] = dot(weights.astype(BF16), grad).astype(BF16)
        upstream = dot(v[rows, cols], grad, NT)
        row_dot = jnp.sum(weights * upstream, axis=0, keepdims=True)
        score = (weights * (upstream - row_dot) * factor).astype(BF16)
        kup = dot(score, qu[pair])
        qup = dot(score, ku[pair], TN)
        for which, (up, normed, inverse, gain, out) in enumerate((
            (qup, qn[pair], qinv[pair], qg_ref[pl.ds(head, 1), :], qgrad_ref),
            (kup, kn[pair], kinv[pair], kg_ref[pl.ds(head, 1), :], kgrad_ref),
        )):
            term = jnp.sum(up * normed, axis=0, keepdims=True)
            old = gains[which][head]
            gains[which][head] = term if old is None else old + term
            out[rows, cols] = norm_backward(up, normed, inverse, gain).astype(BF16)

    for image in range(2):
        remote(
            acc.at[1 - c, part(image)], accr.at[part(image)],
            send_sem.at[12], acc_sem.at[image], core_peer,
        ).start()

    def backward_image(image):
        landed(accr.at[part(image)], acc_sem.at[image])
        for head in range(2):
            backward(image, head)

    stage_y(6)
    stage_mid(10, 1)
    backward_image(0)
    stage_mid(11, 1)
    backward_image(1)
    gown[...] = jnp.zeros_like(gown)
    for which in range(2):
        for head in range(2):
            gown[pl.ds(which * 2 + head, 1), :] = gains[which][head] * (1.0 / 32.0)
    for k in (1, 3, 2):
        remote(gown, gy.at[k - 1], send_sem.at[7], gy_sem, y_peer(k)).start()

    stage_y(8)
    stage_y(10, 1)
    stage_y(11, 1)
    stage_2(0)
    stage_0(6)
    landed(gy, gy_sem)
    gsum[0] = gown[...] + gy[0] + gy[1] + gy[2]
    for k in (1, 2, 3):
        remote(
            gsum.at[0], gz.at[k - 1], send_sem.at[6], gz_sem.at[0], quad_peer(k)
        ).start()
    stage_0(8)
    stage_2(2)
    stage_2(4)
    stage_0(10, 1)
    stage_0(11, 1)
    landed(gz.at[pl.ds(0, 3)], gz_sem.at[0])
    gsum[1] = gsum[0] + gz[0] + gz[1] + gz[2]
    remote(gsum.at[1], gz.at[3], send_sem.at[8], gz_sem.at[1], half_peer).start()
    stage_2(6)
    stage_2(8)
    stage_2(10, 1)
    stage_2(11, 1)
    landed(gz.at[3], gz_sem.at[1])
    total = gsum[1] + gz[3]
    qgg_ref[...] = total[0:2]
    kgg_ref[...] = total[2:4]

    landed(ag.at[pl.ds(0, 2)], send_sem.at[0])
    landed(ag.at[pl.ds(0, 6)], send_sem.at[1])
    landed(w2.at[0], send_sem.at[2])
    landed(att.at[0], send_sem.at[11])
    landed(accr, send_sem.at[12])
    landed(yrecv, send_sem.at[3])
    landed(r0, send_sem.at[4])
    landed(r2, send_sem.at[5])
    landed(gz.at[pl.ds(0, 3)], send_sem.at[6])
    landed(gy, send_sem.at[7])
    landed(gz.at[3], send_sem.at[8])


def place_outputs(*refs):
    for source, target in zip(refs[:6], refs[6:]):
        target[...] = source[...]


def local(cotangent, out_weight, query_raw, key_raw, value, query_gain, key_gain):
    anywhere = pl.BlockSpec(memory_space=pl.ANY)
    vmem = pl.BlockSpec(memory_space=pltpu.VMEM)
    pair = (4, PATCHES, HEAD)
    outs = pl.pallas_call(
        kernel,
        out_shape=(
            jax.ShapeDtypeStruct((TOK, 256), BF16),
            jax.ShapeDtypeStruct((TOK, 256), BF16),
            jax.ShapeDtypeStruct((TOK, 256), BF16),
            jax.ShapeDtypeStruct((8, 6144), BF16),
            jax.ShapeDtypeStruct((2, HEAD), F32),
            jax.ShapeDtypeStruct((2, HEAD), F32),
        ),
        in_specs=[anywhere] * 5 + [vmem] * 2,
        out_specs=[vmem] * 6,
        scratch_shapes=[
            pltpu.VMEM((CHIPS, BLOCKS, TOK, LANES), BF16),
            pltpu.VMEM((BLOCKS, 2, 256, LANES), BF16),
            pltpu.VMEM((2, CHIPS, 256, 384), BF16),
            pltpu.VMEM((TOK, 256), BF16),
            pltpu.VMEM((TOK, 256), BF16),
            pltpu.VMEM((TOK, 256), BF16),
            pltpu.VMEM(pair, F32),
            pltpu.VMEM(pair, F32),
            pltpu.VMEM((4, PATCHES, 1), F32),
            pltpu.VMEM((4, PATCHES, 1), F32),
            pltpu.VMEM(pair, BF16),
            pltpu.VMEM(pair, BF16),
            pltpu.VMEM((4, PATCHES, PATCHES), F32),
            pltpu.VMEM((2, 256, TOK), BF16),
            pltpu.VMEM((2, TOK, 256), F32),
            pltpu.VMEM((TOK, 256), F32),
            pltpu.VMEM((UNITS, NY, NZ, 2, ROWS, LANES), BF16),
            pltpu.VMEM((UNITS, NY - 1, NZ, 2, ROWS, LANES), BF16),
            pltpu.VMEM((NZ, UNITS, 2, ROWS, LANES), BF16),
            pltpu.VMEM((3, 2, UNITS, 2, ROWS, LANES), BF16),
            pltpu.VMEM((2, UNITS, 2, ROWS, LANES), BF16),
            pltpu.VMEM((3, UNITS, ROWS, LANES), BF16),
            pltpu.VMEM((8, LANES), F32),
            pltpu.VMEM((NY - 1, 8, LANES), F32),
            pltpu.VMEM((2, 8, LANES), F32),
            pltpu.VMEM((4, 8, LANES), F32),
            pltpu.SemaphoreType.DMA((4 + BLOCKS,)),
            pltpu.SemaphoreType.DMA((13,)),
            pltpu.SemaphoreType.DMA((BLOCKS, 2)),
            pltpu.SemaphoreType.DMA((BLOCKS, 2)),
            pltpu.SemaphoreType.DMA((CHIPS, BLOCKS)),
            pltpu.SemaphoreType.DMA((2,)),
            pltpu.SemaphoreType.DMA((2,)),
            pltpu.SemaphoreType.DMA((UNITS,)),
            pltpu.SemaphoreType.DMA((UNITS,)),
            pltpu.SemaphoreType.DMA((2, UNITS)),
            pltpu.SemaphoreType.DMA,
            pltpu.SemaphoreType.DMA((2,)),
        ],
        compiler_params=pltpu.CompilerParams(
            collective_id=0, has_side_effects=True, vmem_limit_bytes=60 << 20
        ),
        cost_estimate=pl.CostEstimate(
            flops=4 * 10**9, bytes_accessed=6 * 10**6, transcendentals=4 * 65536
        ),
        name="attention_backward",
    )(cotangent, out_weight, query_raw, key_raw, value, query_gain, key_gain)
    return pl.pallas_call(
        place_outputs,
        out_shape=tuple(jax.ShapeDtypeStruct(out.shape, out.dtype) for out in outs),
        in_specs=[vmem] * 6,
        out_specs=[vmem] * 6,
        compiler_params=pltpu.CompilerParams(vmem_limit_bytes=60 << 20),
        name="place_outputs",
    )(*outs)


def solution(mesh):
    return jax.shard_map(
        local,
        mesh=mesh,
        in_specs=(
            P("dp", "mp"),
            P("mp", None),
            P("dp", "mp"),
            P("dp", "mp"),
            P("dp", "mp"),
            P("mp", None),
            P("mp", None),
        ),
        out_specs=(
            P("dp", "mp"),
            P("dp", "mp"),
            P("dp", "mp"),
            P(("mp", "dp"), None),
            P("mp", None),
            P("mp", None),
        ),
        check_vma=False,
    )
```
